512 devices in a mesh: tgt: 64 (over y, z), sec: 8 (over x, core).
Axes of the slice: x: 4, y: 8, z: 8, core: 2. Of those that a mesh axis runs over, the one named last changes fastest.
Arguments:
- hidden: bfloat16 [384, 16384], P(None, ('sec', 'tgt'))
- norm_gain: bfloat16 [16384], P('sec'), may hold values from 0.5 to 1.5
- vocab_weight: bfloat16 [16384, 65536], P('sec', 'tgt'), may hold values from -0.125 to 0.125
- draft_gain: bfloat16 [16384], replicated, may hold values from 0.5 to 1.5
- query_weight: bfloat16 [16384, 8192], P('sec', 'tgt'), may hold values from -0.046875 to 0.046875
- draft_tokens: int32 [64, 6], P('sec'), may hold values from 0 to 65535
- accepted: int32 [64], P('sec'), may hold values from 0 to 6
- cache_lengths: int32 [64], P('sec'), may hold values from 0 to 1018
Outputs:
- draft_logprob: float32 [64, 6], P('sec')
- draft_query: bfloat16 [384, 8192], P('sec', 'tgt')
The draws below stay inside these ranges and needn't reach their ends.
Inputs may be any that keep to these rules, and one draw needn't show every extreme that they name: cache_lengths[r] + p stays below 1024 for every draft position p.
All inputs are finite; a program needn't handle non-finite values.
Results may differ from the reference program's by a relative error of at most 0.0075.
Values may be sent and summed in bfloat16 or wider, within the bound.
A program may use at most 64 MiB of HBM per device.

```python
import jax
import jax.numpy as jnp
from jax import lax

D = 16384
HD = 128
P_SIZE = 6
MAXPOS = 1024
ROLL = 64
ROWS = 384
V = 65536
HEADS = 64
HQ = 8192


def draw_hidden(key, part):
    key = jax.random.fold_in(key, 11)
    key_base, key_rows, key_cols = jax.random.split(key, 3)
    row_factor = 10.0 ** jax.random.uniform(key_rows, (ROWS, 1), jnp.float32)
    col_factor = 10.0 ** jax.random.uniform(key_cols, (1, D), jnp.float32)
    base = jax.random.normal(key_base, (ROWS, D), jnp.float32)
    values = base * col_factor * row_factor
    return values.astype(jnp.bfloat16)


def with_ends(values, stream_key, low, largest):
    longest = values.shape.index(max(values.shape))
    spots = []
    for shift in (0, 1):
        where = [jax.random.randint(jax.random.fold_in(stream_key, axis), (), 0, length) for axis, length in enumerate(values.shape)]
        where[longest] = (where[longest] + shift) % values.shape[longest]
        spots.append(tuple(where))
    return values.at[spots[0]].set(low).at[spots[1]].set(largest)


def shard_levels(key, shape, cuts, low, largest):
    level = 1.0
    for position, parts in cuts:
        draws = jax.random.uniform(jax.random.fold_in(jax.random.fold_in(key, 6), position), (parts,), jnp.float32, low / len(cuts), largest / len(cuts))
        level = level * jnp.repeat(jnp.exp(draws), shape[position] // parts).reshape((-1,) + (1,) * (len(shape) - 1 - position))
    return level


def scatter_about(stream_key, extent, deviation, limit, cuts=(), kind=jnp.bfloat16):
    factor_of = shard_levels(stream_key, extent, cuts, -0.22, 0.18) if cuts else 1.0
    entries = jax.random.normal(stream_key, extent, jnp.float32) * deviation * factor_of
    return jnp.minimum(jnp.maximum(entries, -limit), limit).astype(kind)


def setup_inputs(seed: int = 0) -> dict:
    keys = jax.random.split(jax.random.key(seed), 9)
    return {
        "hidden": draw_hidden(jax.random.fold_in(keys[8], 71), 0),
        "norm_gain": jnp.clip(1.0 + 0.1 * jax.random.normal(keys[1], (D,), jnp.float32), 0.5, 1.5).astype(jnp.bfloat16),
        "vocab_weight": scatter_about(keys[2], (D, V), (D // 9) ** -0.5, 0.125, ((0, 8), (1, 64))),
        "draft_gain": jnp.clip(1.0 + 0.1 * jax.random.normal(keys[3], (D,), jnp.float32), 0.5, 1.5).astype(jnp.bfloat16),
        "query_weight": scatter_about(keys[4], (D, HQ), D ** -0.5, 0.046875, ((0, 8), (1, 64))),
        "draft_tokens": with_ends(jax.random.randint(keys[5], (ROLL, P_SIZE), 0, V), jax.random.fold_in(keys[5], 1), 0, V - 1).astype(jnp.int32),
        "accepted": with_ends(jax.random.randint(keys[6], (ROLL,), 0, P_SIZE + 1), jax.random.fold_in(keys[6], 1), 0, P_SIZE).astype(jnp.int32),
        "cache_lengths": with_ends(jax.random.randint(keys[7], (ROLL,), 0, MAXPOS - P_SIZE + 1), jax.random.fold_in(keys[7], 1), 0, MAXPOS - P_SIZE).astype(jnp.int32),
    }


def reference(hidden, norm_gain, vocab_weight, draft_gain, query_weight, draft_tokens, accepted, cache_lengths):
    values = hidden.astype(jnp.float32)
    row_scale = lax.rsqrt(lax.optimization_barrier(jnp.mean(values * values, axis=1, keepdims=True)) + 1e-05)
    normed = (values * row_scale * norm_gain.astype(jnp.float32)[None, :]).astype(jnp.bfloat16)
    logits = jnp.dot(normed, vocab_weight, preferred_element_type=jnp.float32)
    totals = lax.optimization_barrier(jnp.sum(jnp.exp(logits), axis=1))
    token_ids = draft_tokens.reshape(-1).astype(jnp.int32)
    picked = jnp.take_along_axis(logits, token_ids[:, None], axis=1)[:, 0]
    draft_logprob = (picked - jnp.log(totals)).reshape(ROLL, P_SIZE)
    draft_normed = (values * row_scale * draft_gain.astype(jnp.float32)[None, :]).astype(jnp.bfloat16)
    query = jnp.dot(draft_normed, query_weight, preferred_element_type=jnp.float32)
    query = query.reshape(ROWS, HEADS, HD)
    half_size = HD // 2
    frequency = jnp.power(jnp.float32(500000.0), -jnp.arange(half_size, dtype=jnp.float32) * 2.0 / HD)
    positions = (cache_lengths[:, None] + jnp.arange(P_SIZE, dtype=jnp.int32)[None, :]).reshape(-1)
    angles = positions.astype(jnp.float32)[:, None] * frequency[None, :]
    cosine = jnp.cos(angles)[:, None, :]
    sine = jnp.sin(angles)[:, None, :]
    first_half = query[:, :, :half_size]
    second_half = query[:, :, half_size:]
    rotated = jnp.concatenate([first_half * cosine - second_half * sine, second_half * cosine + first_half * sine], axis=2)
    accepted_mask = (jnp.arange(P_SIZE, dtype=jnp.int32)[None, :] < accepted[:, None]).reshape(-1)
    rotated = jnp.where(accepted_mask[:, None, None], rotated, jnp.float32(0.0))
    draft_query = rotated.reshape(ROWS, HQ).astype(jnp.bfloat16)
    return (draft_logprob, draft_query)
```

```python
import jax
import jax.numpy as jnp
from jax import lax
from jax.experimental import pallas as pl
from jax.experimental.pallas import tpu as pltpu
from jax.sharding import PartitionSpec as P

D = 16384
HD = 128
RING = 8
MESH = pl.DeviceIdType.MESH


def kernel(
    h_hbm, gain_hbm, w_hbm, dgain_hbm, wq_hbm, tok_ref, accepted_ref, length_ref,
    lp_ref, dq_ref,
    ga, gb, raw, wa, wb, acc, part, landed, sq, sq_in, gains, msg1, msg2, in1, in2,
    local_sem, p1s, p1r, p2s, p2r, rs_s, rs_r, sq_s, sq_r, e1s, e1r, e2s, e2r,
):
    tgt = lax.axis_index("tgt")
    sec = lax.axis_index("sec")
    y, z = tgt // RING, tgt % RING
    rows, vocab = 384, w_hbm.shape[1]
    own = rows // RING

    def z_peer(d):
        return (y * RING + (z + d) % RING, sec)

    def y_peer(d):
        return (((y + d) % RING) * RING + z, sec)

    def s_peer(d):
        return (tgt, (sec + d) % RING)

    w_copies = [
        pltpu.make_async_copy(w_hbm, raw.at[:, pl.ds(0, vocab)], local_sem.at[0]),
        pltpu.make_async_copy(wq_hbm, raw.at[:, pl.ds(vocab, HD)], local_sem.at[1]),
        pltpu.make_async_copy(gain_hbm, gains.at[0], local_sem.at[2]),
        pltpu.make_async_copy(dgain_hbm.at[pl.ds(sec * 16, 16)], gains.at[1], local_sem.at[3]),
    ]
    h_copies = [
        pltpu.make_async_copy(h_hbm.at[pl.ds(0, 16)], ga.at[y, z], local_sem.at[4]),
        pltpu.make_async_copy(h_hbm.at[pl.ds(16, 16)], gb.at[z, y], local_sem.at[5]),
    ]
    for c in h_copies + w_copies:
        c.start()

    barrier = pltpu.get_barrier_semaphore()
    for d in range(1, RING):
        for peer in (z_peer(d), y_peer(d), s_peer(d)):
            pl.semaphore_signal(barrier, inc=1, device_id=peer, device_id_type=MESH)
    pl.semaphore_wait(barrier, 3 * (RING - 1))

    first = []
    for d in range(1, RING):
        first.append(pltpu.make_async_remote_copy(
            h_hbm.at[pl.ds(0, 16)], ga.at[y, z], p1s.at[0, d], p1r.at[0, d],
            device_id=z_peer(d), device_id_type=MESH))
        first.append(pltpu.make_async_remote_copy(
            h_hbm.at[pl.ds(16, 16)], gb.at[z, y], p1s.at[1, d], p1r.at[1, d],
            device_id=y_peer(d), device_id_type=MESH))
    for c in first:
        c.start()
    for c in h_copies:
        c.wait()
    for c in first:
        c.wait_recv()

    def ring_copies(s):
        out = []
        for k, (buf, at, peer) in enumerate(((ga, y, y_peer), (gb, z, z_peer))):
            for way in (0, 1):
                step = 1 if way == 0 else -1
                block = (at - step * (s - 1)) % RING if s > 1 else at
                ref = buf.at[block]
                if s == 4:
                    ref = buf.at[block, pl.ds(4 * way, 4)]
                out.append(pltpu.make_async_remote_copy(
                    ref, ref, p2s.at[k, way, s - 1], p2r.at[k, way, s - 1],
                    device_id=peer(step), device_id_type=MESH))
        return out

    second = [ring_copies(s) for s in range(1, 5)]
    for c in second[0]:
        c.start()

    for c in w_copies:
        c.wait()
    gt = jnp.transpose(gains[0].astype(jnp.float32))
    dgt = jnp.transpose(gains[1].astype(jnp.float32))
    for j in range(16):
        span = pl.ds(128 * j, 128)
        left = (raw[span, pl.ds(0, vocab)].astype(jnp.float32) * gt[:, j:j + 1]).astype(jnp.bfloat16)
        right = (raw[span, pl.ds(vocab, HD)].astype(jnp.float32) * dgt[:, j:j + 1]).astype(jnp.bfloat16)
        for i in range(4):
            yy, zz = j // 2, 4 * (j % 2) + i
            for wide, values in ((pl.ds(0, vocab), left), (pl.ds(vocab, HD), right)):
                wa[yy, zz, :, wide] = values[32 * i:32 * i + 16]
                wb[zz, yy, :, wide] = values[32 * i + 16:32 * i + 32]

    def take(h_parts, w_parts, fresh):
        h = jnp.concatenate([v.reshape(128, rows) for v in h_parts], axis=0)
        hf = h.astype(jnp.float32)
        squares = jnp.sum((hf * hf).reshape(32, 8, rows), axis=0)
        sq[...] = squares if fresh else sq[...] + squares
        ht = jnp.transpose(h)
        for n in range(3):
            cols = pl.ds(n * 384, 384)
            w = jnp.concatenate([r[b, :, :, cols].reshape(128, 384) for r, b in w_parts], axis=0)
            prod = jnp.dot(ht, w, preferred_element_type=jnp.float32)
            if fresh:
                acc[:, cols] = prod
            else:
                acc[:, cols] += prod

    take([ga[y], gb[z]], [(wa, y), (wb, z)], True)
    for s in range(1, 4):
        for c in second[s - 1]:
            c.wait_recv()
        for c in second[s]:
            c.start()
        for buf, w, at in ((ga, wa, y), (gb, wb, z)):
            b1, b2 = (at + s) % RING, (at + RING - s) % RING
            take([buf[b1], buf[b2]], [(w, b1), (w, b2)], False)
    for c in second[3]:
        c.wait_recv()
    far_y, far_z = (y + 4) % RING, (z + 4) % RING
    take([ga[far_y], gb[far_z]], [(wa, far_y), (wb, far_z)], False)

    sq_copies, rs_copies = [], []
    sq_in[sec] = sq[...]
    for d in range(1, RING):
        sq_copies.append(pltpu.make_async_remote_copy(
            sq, sq_in.at[sec], sq_s.at[d], sq_r.at[d], device_id=s_peer(d), device_id_type=MESH))
        rs_copies.append(pltpu.make_async_remote_copy(
            part.at[(sec + d) % RING], landed.at[sec], rs_s.at[d], rs_r.at[d],
            device_id=s_peer(d), device_id_type=MESH))
    for c in sq_copies:
        c.start()
    for d in range(1, RING):
        to = (sec + d) % RING
        part[to] = acc[pl.ds(to * own, own), :].astype(jnp.bfloat16)
        rs_copies[d - 1].start()

    row8 = lax.broadcasted_iota(jnp.int32, (own, 8), 0)
    lane6 = lax.broadcasted_iota(jnp.int32, (own, 6), 1)
    row6 = lax.broadcasted_iota(jnp.int32, (own, 6), 0)
    row1 = row8[:, :1]
    place = jnp.zeros((own, 1), jnp.int32)
    length = jnp.zeros((own, 1), jnp.int32)
    limit = jnp.zeros((own, 1), jnp.int32)
    token6 = jnp.zeros((own, 6), jnp.int32)
    for r in range(8):
        inside = (row1 >= 6 * r) & (row1 < 6 * r + 6)
        place = jnp.where(inside, row1 - 6 * r, place)
        length = jnp.where(inside, length_ref[r], length)
        limit = jnp.where(inside, accepted_ref[r], limit)
        token6 = jnp.where(row6 == lane6 + 6 * r, jnp.broadcast_to(tok_ref[pl.ds(r, 1), :], (own, 6)), token6)
    token = jnp.sum(token6.astype(jnp.float32), axis=1, keepdims=True).astype(jnp.int32)
    unit = lax.broadcasted_iota(jnp.int32, (own, HD), 1)
    half = jnp.where(unit >= HD // 2, unit - HD // 2, unit).astype(jnp.float32)
    frequency = jnp.exp(half * jnp.float32(-2.0 / HD * 13.122363377404328))
    angle = (length + place).astype(jnp.float32) * frequency
    cosine = jnp.cos(angle)
    sine = jnp.where(unit < HD // 2, -jnp.sin(angle), jnp.sin(angle))

    for c in sq_copies:
        c.wait_recv()
    squares = jnp.sum(jnp.sum(sq_in[...], axis=0), axis=0, keepdims=True)
    scale_row = lax.rsqrt(squares / D + 1e-05)
    lane = lax.broadcasted_iota(jnp.int32, (own, rows), 1)
    sub = lax.broadcasted_iota(jnp.int32, (own, rows), 0)
    scale = jnp.sum(jnp.where(lane == sub + sec * own, scale_row, 0.0), axis=1, keepdims=True)

    total = acc[pl.ds(sec * own, own), :]
    for d in range(1, RING):
        rs_copies[d - 1].wait_recv()
        total = total + landed[(sec + RING - d) % RING].astype(jnp.float32)
    full = jnp.where(scale == 0.0, 0.0, total * scale)
    logits = full[:, :vocab]
    query = full[:, vocab:]
    ids = lax.broadcasted_iota(jnp.int32, (own, vocab), 1) + tgt * vocab
    picked = jnp.sum(jnp.where(ids == token, logits, 0.0), axis=1, keepdims=True)
    exps = jnp.sum(jnp.exp(logits), axis=1, keepdims=True)
    eye = lax.broadcasted_iota(jnp.int32, (own, 128), 0) == lax.broadcasted_iota(jnp.int32, (own, 128), 1)
    exp_row = jnp.sum(jnp.where(eye, exps, 0.0), axis=0, keepdims=True)
    pick_row = jnp.sum(jnp.where(eye, picked, 0.0), axis=0, keepdims=True)
    which = lax.broadcasted_iota(jnp.int32, (8, 128), 0)
    msg1[...] = jnp.where(which == 0, exp_row, jnp.where(which == 1, pick_row, 0.0))

    def exchange(msg, inbox, at, peer, ssem, rsem):
        copies = [pltpu.make_async_remote_copy(
            msg, inbox.at[at], ssem.at[d], rsem.at[d], device_id=peer(d), device_id_type=MESH)
            for d in range(1, RING)]
        for c in copies:
            c.start()
        inbox[at] = msg[...]
        return copies

    e1 = exchange(msg1, in1, z, z_peer, e1s, e1r)
    rotated = query * cosine + pltpu.roll(query, HD // 2, 1) * sine
    dq_ref[...] = jnp.where(place < limit, rotated, 0.0).astype(jnp.bfloat16)
    for c in e1:
        c.wait_recv()
    msg2[...] = jnp.sum(in1[...], axis=0)
    e2 = exchange(msg2, in2, y, y_peer, e2s, e2r)
    for c in e2:
        c.wait_recv()
    sums = jnp.sum(in2[...], axis=0)
    lp_row = sums[1:2] - jnp.log(sums[0:1])
    sub8 = lax.broadcasted_iota(jnp.int32, (8, 128), 0)
    lane8 = lax.broadcasted_iota(jnp.int32, (8, 128), 1)
    out_lane = lax.broadcasted_iota(jnp.int32, (8, 6), 1)
    out = jnp.zeros((8, 6), jnp.float32)
    for p in range(6):
        col = jnp.sum(jnp.where(lane8 == 6 * sub8 + p, lp_row, 0.0), axis=1, keepdims=True)
        out = jnp.where(out_lane == p, col, out)
    lp_ref[...] = out

    for c in first + sum(second, []) + sq_copies + rs_copies + e1 + e2:
        c.wait_send()


def local(
    hidden, norm_gain, vocab_weight, draft_gain, query_weight, draft_tokens, accepted, cache_lengths
):
    rows, vocab = hidden.shape[0], vocab_weight.shape[1]
    wide = vocab + HD
    depth = vocab_weight.shape[0]
    own = rows // RING
    any_spec = pl.BlockSpec(memory_space=pl.ANY)
    vmem, smem = pl.BlockSpec(memory_space=pltpu.VMEM), pl.BlockSpec(memory_space=pltpu.SMEM)
    bf16, f32 = jnp.bfloat16, jnp.float32
    dma = pltpu.SemaphoreType.DMA
    lp, dq = pl.pallas_call(
        kernel,
        out_shape=(
            jax.ShapeDtypeStruct(draft_tokens.shape, f32),
            jax.ShapeDtypeStruct((own, HD), bf16),
        ),
        in_specs=[any_spec] * 5 + [vmem, smem, smem],
        out_specs=(vmem, vmem),
        scratch_shapes=[
            pltpu.VMEM((8, 8, 16, rows), bf16),
            pltpu.VMEM((8, 8, 16, rows), bf16),
            pltpu.VMEM((depth, wide), bf16),
            pltpu.VMEM((8, 8, 16, wide), bf16),
            pltpu.VMEM((8, 8, 16, wide), bf16),
            pltpu.VMEM((rows, wide), f32),
            pltpu.VMEM((8, own, wide), bf16),
            pltpu.VMEM((8, own, wide), bf16),
            pltpu.VMEM((8, rows), f32),
            pltpu.VMEM((8, 8, rows), f32),
            pltpu.VMEM((2, 16, 128), bf16),
            pltpu.VMEM((8, 128), f32),
            pltpu.VMEM((8, 128), f32),
            pltpu.VMEM((8, 8, 128), f32),
            pltpu.VMEM((8, 8, 128), f32),
            dma((6,)),
            dma((2, 8)), dma((2, 8)),
            dma((2, 2, 4)), dma((2, 2, 4)),
            dma((8,)), dma((8,)),
            dma((8,)), dma((8,)),
            dma((8,)), dma((8,)),
            dma((8,)), dma((8,)),
        ],
        compiler_params=pltpu.CompilerParams(
            collective_id=0, has_side_effects=True, vmem_limit_bytes=40 * 1024 * 1024
        ),
    )(
        hidden.T,
        norm_gain.reshape(16, 128),
        vocab_weight,
        draft_gain.reshape(128, 128),
        query_weight,
        draft_tokens,
        accepted,
        cache_lengths,
    )
    return lp, dq


def solution(mesh):
    return jax.shard_map(
        local,
        mesh=mesh,
        in_specs=(
            P(None, ("sec", "tgt")),
            P("sec"),
            P("sec", "tgt"),
            P(),
            P("sec", "tgt"),
            P("sec", None),
            P("sec"),
            P("sec"),
        ),
        out_specs=(P("sec", None), P("sec", "tgt")),
        check_vma=False,
    )
```

```python
import jax
import jax.numpy as jnp
from jax import lax
from jax.experimental import pallas as pl
from jax.experimental.pallas import tpu as pltpu
from jax.sharding import PartitionSpec as P

D = 16384
HD = 128
RING = 8
MESH = pl.DeviceIdType.MESH
SLOT = (0, 1, 3, 5, 7, 6, 4, 2)
PARTS = ((0, 3, 2), (3, 5, 2))


def kernel(
    h_hbm, gain_hbm, w_hbm, dgain_hbm, wq_hbm, tok_ref, accepted_ref, length_ref,
    lp_ref, dq_ref,
    ga, gb, raw, wa, wb, acc, mine, part, landed, sq, sq_pair, sq_in, gains, msg1, msg2, in1, in2,
    local_sem, p1s, p1r, p2s, p2r, rs_s, rs_r, sq_s, sq_r, e1s, e1r, e2s, e2r,
):
    tgt = lax.axis_index("tgt")
    sec = lax.axis_index("sec")
    y, z = tgt // RING, tgt % RING
    rows, vocab = 384, w_hbm.shape[1]
    own = rows // RING

    def z_peer(d):
        return (y * RING + (z + d) % RING, sec)

    def y_peer(d):
        return (((y + d) % RING) * RING + z, sec)

    x, core = sec // 2, sec % 2
    sibling = (tgt, 2 * x + 1 - core)

    def x_peer(d):
        return (tgt, 2 * ((x + d) % 4) + core)

    barrier = pltpu.get_barrier_semaphore()
    for d in (4, 3, 5, 2, 6, 1, 7):
        for peer in (z_peer(d), y_peer(d)):
            pl.semaphore_signal(barrier, inc=1, device_id=peer, device_id_type=MESH)
    for peer in (sibling, x_peer(1), x_peer(2), x_peer(3)):
        pl.semaphore_signal(barrier, inc=1, device_id=peer, device_id_type=MESH)

    w_copies = [
        pltpu.make_async_copy(w_hbm, raw.at[:, pl.ds(0, vocab)], local_sem.at[0]),
        pltpu.make_async_copy(wq_hbm, raw.at[:, pl.ds(vocab, HD)], local_sem.at[1]),
        pltpu.make_async_copy(gain_hbm, gains.at[0], local_sem.at[2]),
        pltpu.make_async_copy(dgain_hbm.at[pl.ds(sec * 16, 16)], gains.at[1], local_sem.at[3]),
    ]
    h_copies = [
        pltpu.make_async_copy(h_hbm.at[pl.ds(0, 16)], ga.at[y, 0], local_sem.at[4]),
        pltpu.make_async_copy(h_hbm.at[pl.ds(16, 16)], gb.at[z, 0], local_sem.at[5]),
    ]
    for c in h_copies + w_copies:
        c.start()

    pl.semaphore_wait(barrier, 2 * (RING - 1) + 4)

    def first_copies(d):
        to = SLOT[RING - d]
        return [
            pltpu.make_async_remote_copy(
                h_hbm.at[pl.ds(0, 16)], ga.at[y, to], p1s.at[0, d], p1r.at[0, d],
                device_id=z_peer(d), device_id_type=MESH),
            pltpu.make_async_remote_copy(
                h_hbm.at[pl.ds(16, 16)], gb.at[z, to], p1s.at[1, d], p1r.at[1, d],
                device_id=y_peer(d), device_id_type=MESH),
        ]

    first = {d: first_copies(d) for d in range(1, RING)}
    for d in (1, 7, 2, 6, 3, 5, 4):
        for c in first[d]:
            c.start()

    def ring_copies(p):
        at_slot, count, up = PARTS[p]
        near, far, third, fourth = [], [], [], []
        for k, (buf, at, peer) in enumerate(((ga, y, y_peer), (gb, z, z_peer))):
            for way in (0, 1):
                step = 1 if way == 0 else RING - 1
                from2 = (at + 2 * (RING - step)) % RING
                lo, n = (at_slot, up) if way == 0 else (at_slot + up, count - up)
                for kind, (group, ref, hops) in enumerate((
                    (near, buf.at[at, pl.ds(at_slot, count)], step),
                    (far, buf.at[at, pl.ds(at_slot, count)], 2 * step),
                    (third, buf.at[from2, pl.ds(at_slot, count)], step),
                    (fourth, buf.at[from2, pl.ds(lo, n)] if n else None, 2 * step),
                )):
                    if ref is not None:
                        group.append(pltpu.make_async_remote_copy(
                            ref, ref, p2s.at[p, k, way, kind], p2r.at[p, k, way, kind],
                            device_id=peer(hops), device_id_type=MESH))
        return near, far, third, fourth

    second = [ring_copies(p) for p in range(len(PARTS))]

    def spread(p):
        for slot in range(PARTS[p][0], PARTS[p][0] + PARTS[p][1]):
            if slot > 0:
                for c in first[RING - SLOT.index(slot)]:
                    c.wait_recv()
        for c in second[p][1] + second[p][0]:
            c.start()

    def pass_on(p):
        for c in second[p][1]:
            c.wait_recv()
        for c in second[p][3] + second[p][2]:
            c.start()

    def arrived(kind):
        for group in second:
            for c in group[kind]:
                c.wait_recv()

    for c in h_copies:
        c.wait()
    for p in range(len(PARTS)):
        spread(p)

    for c in w_copies:
        c.wait()

    def slot_of(rel):
        return jnp.where(rel == 0, 0, jnp.where(rel <= 4, 2 * rel - 1, 16 - 2 * rel))

    gt = jnp.transpose(gains[0].astype(jnp.float32))
    dgt = jnp.transpose(gains[1].astype(jnp.float32))
    for j in range(16):
        span = pl.ds(128 * j, 128)
        left = (raw[span, pl.ds(0, vocab)].astype(jnp.float32) * gt[:, j:j + 1]).astype(jnp.bfloat16)
        right = (raw[span, pl.ds(vocab, HD)].astype(jnp.float32) * dgt[:, j:j + 1]).astype(jnp.bfloat16)
        for i in range(4):
            yy, zz = j // 2, 4 * (j % 2) + i
            for wide, values in ((pl.ds(0, vocab), left), (pl.ds(vocab, HD), right)):
                wa[yy, slot_of((zz + RING - z) % RING), :, wide] = values[32 * i:32 * i + 16]
                wb[zz, slot_of((yy + RING - y) % RING), :, wide] = values[32 * i + 16:32 * i + 32]

    def take(h_parts, w_parts, fresh):
        h = jnp.concatenate([v.reshape(128, rows) for v in h_parts], axis=0)
        hf = h.astype(jnp.float32)
        squares = jnp.sum((hf * hf).reshape(32, 8, rows), axis=0)
        sq[...] = squares if fresh else sq[...] + squares
        ht = jnp.transpose(h)
        for n in range(3):
            cols = pl.ds(n * 384, 384)
            w = jnp.concatenate([r[b, :, :, cols].reshape(128, 384) for r, b in w_parts], axis=0)
            prod = jnp.dot(ht, w, preferred_element_type=jnp.float32)
            if fresh:
                acc[:, cols] = prod
            else:
                acc[:, cols] += prod

    take([ga[y], gb[z]], [(wa, y), (wb, z)], True)
    def take_pair(s):
        for buf, w, at in ((ga, wa, y), (gb, wb, z)):
            b1, b2 = (at + s) % RING, (at + RING - s) % RING
            take([buf[b1], buf[b2]], [(w, b1), (w, b2)], False)

    for p in range(len(PARTS)):
        pass_on(p)
    arrived(0)
    take_pair(1)
    take_pair(2)
    arrived(2)
    take_pair(3)
    arrived(3)
    far_y, far_z = (y + 4) % RING, (z + 4) % RING
    take([ga[far_y], gb[far_z]], [(wa, far_y), (wb, far_z)], False)

    order = (2, 1, 3, 0)
    pair_sq = pltpu.make_async_remote_copy(
        sq, sq_in.at[0], sq_s.at[0], sq_r.at[0], device_id=sibling, device_id_type=MESH)
    pair_sq.start()
    pair_copies, x_copies, x_sq = [], [], []
    for i, d in enumerate(order):
        pair_copies.append(pltpu.make_async_remote_copy(
            part.at[i], landed.at[i], rs_s.at[i], rs_r.at[i], device_id=sibling, device_id_type=MESH))
        if d:
            x_copies.append(pltpu.make_async_remote_copy(
                part.at[4 + i], landed.at[4 + i], rs_s.at[4 + i], rs_r.at[4 + i],
                device_id=x_peer(d), device_id_type=MESH))
            x_sq.append(pltpu.make_async_remote_copy(
                sq_pair, sq_in.at[d], sq_s.at[d], sq_r.at[d],
                device_id=x_peer(d), device_id_type=MESH))

    def rows_of(d, side):
        return pl.ds((2 * ((x + d) % 4) + side) * own, own)

    for i, d in enumerate(order):
        part[i] = acc[rows_of(d, 1 - core), :].astype(jnp.bfloat16)
        pair_copies[i].start()
    pair_sq.wait_recv()
    sq_pair[...] = sq[...] + sq_in[0]
    for c in x_sq:
        c.start()
    for i, d in enumerate(order):
        pair_copies[i].wait_recv()
        both = acc[rows_of(d, core), :] + landed[i].astype(jnp.float32)
        if d:
            part[4 + i] = both.astype(jnp.bfloat16)
            x_copies[i].start()
        else:
            mine[...] = both

    row8 = lax.broadcasted_iota(jnp.int32, (own, 8), 0)
    lane6 = lax.broadcasted_iota(jnp.int32, (own, 6), 1)
    row6 = lax.broadcasted_iota(jnp.int32, (own, 6), 0)
    row1 = row8[:, :1]
    place = jnp.zeros((own, 1), jnp.int32)
    length = jnp.zeros((own, 1), jnp.int32)
    limit = jnp.zeros((own, 1), jnp.int32)
    token6 = jnp.zeros((own, 6), jnp.int32)
    for r in range(8):
        inside = (row1 >= 6 * r) & (row1 < 6 * r + 6)
        place = jnp.where(inside, row1 - 6 * r, place)
        length = jnp.where(inside, length_ref[r], length)
        limit = jnp.where(inside, accepted_ref[r], limit)
        token6 = jnp.where(row6 == lane6 + 6 * r, jnp.broadcast_to(tok_ref[pl.ds(r, 1), :], (own, 6)), token6)
    token = jnp.sum(token6.astype(jnp.float32), axis=1, keepdims=True).astype(jnp.int32)
    unit = lax.broadcasted_iota(jnp.int32, (own, HD), 1)
    half = jnp.where(unit >= HD // 2, unit - HD // 2, unit).astype(jnp.float32)
    frequency = jnp.exp(half * jnp.float32(-2.0 / HD * 13.122363377404328))
    angle = (length + place).astype(jnp.float32) * frequency
    cosine = jnp.cos(angle)
    sine = jnp.where(unit < HD // 2, -jnp.sin(angle), jnp.sin(angle))

    for c in x_sq:
        c.wait_recv()
    squares = sq_pair[...] + sq_in[1] + sq_in[2] + sq_in[3]
    squares = jnp.sum(squares, axis=0, keepdims=True)
    scale_row = lax.rsqrt(squares / D + 1e-05)
    lane = lax.broadcasted_iota(jnp.int32, (own, rows), 1)
    sub = lax.broadcasted_iota(jnp.int32, (own, rows), 0)
    scale = jnp.sum(jnp.where(lane == sub + sec * own, scale_row, 0.0), axis=1, keepdims=True)

    total = mine[...]
    for i in range(3):
        x_copies[i].wait_recv()
        total = total + landed[4 + i].astype(jnp.float32)
    full = jnp.where(scale == 0.0, 0.0, total * scale)
    logits = full[:, :vocab]
    query = full[:, vocab:]
    ids = lax.broadcasted_iota(jnp.int32, (own, vocab), 1) + tgt * vocab
    picked = jnp.sum(jnp.where(ids == token, logits, 0.0), axis=1, keepdims=True)
    exps = jnp.sum(jnp.exp(logits), axis=1, keepdims=True)
    eye = lax.broadcasted_iota(jnp.int32, (own, 128), 0) == lax.broadcasted_iota(jnp.int32, (own, 128), 1)
    exp_row = jnp.sum(jnp.where(eye, exps, 0.0), axis=0, keepdims=True)
    pick_row = jnp.sum(jnp.where(eye, picked, 0.0), axis=0, keepdims=True)
    which = lax.broadcasted_iota(jnp.int32, (8, 128), 0)
    msg1[...] = jnp.where(which == 0, exp_row, jnp.where(which == 1, pick_row, 0.0))

    def exchange(msg, inbox, at, peer, ssem, rsem):
        copies = [pltpu.make_async_remote_copy(
            msg, inbox.at[at], ssem.at[d], rsem.at[d], device_id=peer(d), device_id_type=MESH)
            for d in range(1, RING)]
        for c in copies:
            c.start()
        inbox[at] = msg[...]
        return copies

    e1 = exchange(msg1, in1, z, z_peer, e1s, e1r)
    rotated = query * cosine + pltpu.roll(query, HD // 2, 1) * sine
    dq_ref[...] = jnp.where(place < limit, rotated, 0.0).astype(jnp.bfloat16)
    for c in e1:
        c.wait_recv()
    msg2[...] = jnp.sum(in1[...], axis=0)
    e2 = exchange(msg2, in2, y, y_peer, e2s, e2r)
    for c in e2:
        c.wait_recv()
    sums = jnp.sum(in2[...], axis=0)
    lp_row = sums[1:2] - jnp.log(sums[0:1])
    sub8 = lax.broadcasted_iota(jnp.int32, (8, 128), 0)
    lane8 = lax.broadcasted_iota(jnp.int32, (8, 128), 1)
    out_lane = lax.broadcasted_iota(jnp.int32, (8, 6), 1)
    out = jnp.zeros((8, 6), jnp.float32)
    for p in range(6):
        col = jnp.sum(jnp.where(lane8 == 6 * sub8 + p, lp_row, 0.0), axis=1, keepdims=True)
        out = jnp.where(out_lane == p, col, out)
    lp_ref[...] = out

    for c in sum(first.values(), []) + sum([sum(g, []) for g in second], []) + [pair_sq] + x_sq + pair_copies + x_copies + e1 + e2:
        c.wait_send()


def local(
    hidden, norm_gain, vocab_weight, draft_gain, query_weight, draft_tokens, accepted, cache_lengths
):
    rows, vocab = hidden.shape[0], vocab_weight.shape[1]
    wide = vocab + HD
    depth = vocab_weight.shape[0]
    own = rows // RING
    any_spec = pl.BlockSpec(memory_space=pl.ANY)
    vmem, smem = pl.BlockSpec(memory_space=pltpu.VMEM), pl.BlockSpec(memory_space=pltpu.SMEM)
    bf16, f32 = jnp.bfloat16, jnp.float32
    dma = pltpu.SemaphoreType.DMA
    lp, dq = pl.pallas_call(
        kernel,
        out_shape=(
            jax.ShapeDtypeStruct(draft_tokens.shape, f32),
            jax.ShapeDtypeStruct((own, HD), bf16),
        ),
        in_specs=[any_spec] * 5 + [vmem, smem, smem],
        out_specs=(vmem, vmem),
        scratch_shapes=[
            pltpu.VMEM((8, 8, 16, rows), bf16),
            pltpu.VMEM((8, 8, 16, rows), bf16),
            pltpu.VMEM((depth, wide), bf16),
            pltpu.VMEM((8, 8, 16, wide), bf16),
            pltpu.VMEM((8, 8, 16, wide), bf16),
            pltpu.VMEM((rows, wide), f32),
            pltpu.VMEM((own, wide), f32),
            pltpu.VMEM((8, own, wide), bf16),
            pltpu.VMEM((8, own, wide), bf16),
            pltpu.VMEM((8, rows), f32),
            pltpu.VMEM((8, rows), f32),
            pltpu.VMEM((4, 8, rows), f32),
            pltpu.VMEM((2, 16, 128), bf16),
            pltpu.VMEM((8, 128), f32),
            pltpu.VMEM((8, 128), f32),
            pltpu.VMEM((8, 8, 128), f32),
            pltpu.VMEM((8, 8, 128), f32),
            dma((6,)),
            dma((2, 8)), dma((2, 8)),
            dma((len(PARTS), 2, 2, 4)), dma((len(PARTS), 2, 2, 4)),
            dma((8,)), dma((8,)),
            dma((8,)), dma((8,)),
            dma((8,)), dma((8,)),
            dma((8,)), dma((8,)),
        ],
        compiler_params=pltpu.CompilerParams(
            collective_id=0, has_side_effects=True, vmem_limit_bytes=60 * 1024 * 1024
        ),
    )(
        hidden.T,
        norm_gain.reshape(16, 128),
        vocab_weight,
        draft_gain.reshape(128, 128),
        query_weight,
        draft_tokens,
        accepted,
        cache_lengths,
    )
    return lp, dq


def solution(mesh):
    return jax.shard_map(
        local,
        mesh=mesh,
        in_specs=(
            P(None, ("sec", "tgt")),
            P("sec"),
            P("sec", "tgt"),
            P(),
            P("sec", "tgt"),
            P("sec", None),
            P("sec"),
            P("sec"),
        ),
        out_specs=(P("sec", None), P("sec", "tgt")),
        check_vma=False,
    )
```

```python
import jax
import jax.numpy as jnp
from jax import lax
from jax.experimental import pallas as pl
from jax.experimental.pallas import tpu as pltpu
from jax.sharding import PartitionSpec as P

D = 16384
HD = 128
RING = 8
MESH = pl.DeviceIdType.MESH
SLOT = (0, 1, 3, 5, 7, 6, 4, 2)
PARTS = ((0, 3, 2), (3, 5, 2))


def kernel(
    h_hbm, gain_hbm, w_hbm, dgain_hbm, wq_hbm, tok_ref, accepted_ref, length_ref,
    lp_ref, dq_ref,
    ga, gb, raw, wa, wb, acc, mine, part, landed, sq, sq_own, sq_pair, sq_in, gains, msg1, msg2, in1, in2,
    local_sem, p1s, p1r, p2s, p2r, rs_s, rs_r, sq_s, sq_r, e1s, e1r, e2s, e2r,
):
    tgt = lax.axis_index("tgt")
    sec = lax.axis_index("sec")
    y, z = tgt // RING, tgt % RING
    rows, vocab = 384, w_hbm.shape[1]
    own = rows // RING

    def z_peer(d):
        return (y * RING + (z + d) % RING, sec)

    def y_peer(d):
        return (((y + d) % RING) * RING + z, sec)

    x, core = sec // 2, sec % 2
    sibling = (tgt, 2 * x + 1 - core)

    def x_peer(d):
        return (tgt, 2 * ((x + d) % 4) + core)

    barrier = pltpu.get_barrier_semaphore()
    for d in (4, 3, 5, 2, 6, 1, 7):
        for peer in (z_peer(d), y_peer(d)):
            pl.semaphore_signal(barrier, inc=1, device_id=peer, device_id_type=MESH)
    for peer in (sibling, x_peer(1), x_peer(2), x_peer(3)):
        pl.semaphore_signal(barrier, inc=1, device_id=peer, device_id_type=MESH)

    w_copies = [
        pltpu.make_async_copy(w_hbm, raw.at[:, pl.ds(0, vocab)], local_sem.at[0]),
        pltpu.make_async_copy(wq_hbm, raw.at[:, pl.ds(vocab, HD)], local_sem.at[1]),
        pltpu.make_async_copy(gain_hbm, gains.at[0], local_sem.at[2]),
        pltpu.make_async_copy(dgain_hbm.at[pl.ds(sec * 16, 16)], gains.at[1], local_sem.at[3]),
    ]
    h_copies = [
        pltpu.make_async_copy(h_hbm.at[pl.ds(0, 16)], ga.at[y, 0], local_sem.at[4]),
        pltpu.make_async_copy(h_hbm.at[pl.ds(16, 16)], gb.at[z, 0], local_sem.at[5]),
    ]
    for c in h_copies + w_copies:
        c.start()

    pl.semaphore_wait(barrier, 2 * (RING - 1) + 4)

    def first_copies(d):
        to = SLOT[RING - d]
        return [
            pltpu.make_async_remote_copy(
                h_hbm.at[pl.ds(0, 16)], ga.at[y, to], p1s.at[0, d], p1r.at[0, d],
                device_id=z_peer(d), device_id_type=MESH),
            pltpu.make_async_remote_copy(
                h_hbm.at[pl.ds(16, 16)], gb.at[z, to], p1s.at[1, d], p1r.at[1, d],
                device_id=y_peer(d), device_id_type=MESH),
        ]

    first = {d: first_copies(d) for d in range(1, RING)}
    for d in (1, 7, 2, 6, 3, 5, 4):
        for c in first[d]:
            c.start()

    def ring_copies(p):
        at_slot, count, up = PARTS[p]
        near, far, third, fourth = [], [], [], []
        for k, (buf, at, peer) in enumerate(((ga, y, y_peer), (gb, z, z_peer))):
            for way in (0, 1):
                step = 1 if way == 0 else RING - 1
                from2 = (at + 2 * (RING - step)) % RING
                lo, n = (at_slot, up) if way == 0 else (at_slot + up, count - up)
                for kind, (group, ref, hops) in enumerate((
                    (near, buf.at[at, pl.ds(at_slot, count)], step),
                    (far, buf.at[at, pl.ds(at_slot, count)], 2 * step),
                    (third, buf.at[from2, pl.ds(at_slot, count)], step),
                    (fourth, buf.at[from2, pl.ds(lo, n)] if n else None, 2 * step),
                )):
                    if ref is not None:
                        group.append(pltpu.make_async_remote_copy(
                            ref, ref, p2s.at[p, k, way, kind], p2r.at[p, k, way, kind],
                            device_id=peer(hops), device_id_type=MESH))
        return near, far, third, fourth

    second = [ring_copies(p) for p in range(len(PARTS))]

    def spread(p):
        for slot in range(PARTS[p][0], PARTS[p][0] + PARTS[p][1]):
            if slot > 0:
                for c in first[RING - SLOT.index(slot)]:
                    c.wait_recv()
        for c in second[p][1] + second[p][0]:
            c.start()

    def pass_on(p):
        for c in second[p][1]:
            c.wait_recv()
        for c in second[p][3] + second[p][2]:
            c.start()

    def arrived(kind):
        for group in second:
            for c in group[kind]:
                c.wait_recv()

    for c in h_copies:
        c.wait()
    for p in range(len(PARTS)):
        spread(p)

    for c in w_copies:
        c.wait()

    def slot_of(rel):
        return jnp.where(rel == 0, 0, jnp.where(rel <= 4, 2 * rel - 1, 16 - 2 * rel))

    gt = jnp.transpose(gains[0].astype(jnp.float32))
    dgt = jnp.transpose(gains[1].astype(jnp.float32))
    for j in range(16):
        span = pl.ds(128 * j, 128)
        left = (raw[span, pl.ds(0, vocab)].astype(jnp.float32) * gt[:, j:j + 1]).astype(jnp.bfloat16)
        right = (raw[span, pl.ds(vocab, HD)].astype(jnp.float32) * dgt[:, j:j + 1]).astype(jnp.bfloat16)
        for i in range(4):
            yy, zz = j // 2, 4 * (j % 2) + i
            for wide, values in ((pl.ds(0, vocab), left), (pl.ds(vocab, HD), right)):
                wa[yy, slot_of((zz + RING - z) % RING), :, wide] = values[32 * i:32 * i + 16]
                wb[zz, slot_of((yy + RING - y) % RING), :, wide] = values[32 * i + 16:32 * i + 32]

    def take(h_parts, w_parts, fresh):
        h = jnp.concatenate([v.reshape(128, rows) for v in h_parts], axis=0)
        hf = h.astype(jnp.float32)
        squares = jnp.sum((hf * hf).reshape(32, 8, rows), axis=0)
        sq[...] = squares if fresh else sq[...] + squares
        ht = jnp.transpose(h)
        for n in range(3):
            cols = pl.ds(n * 384, 384)
            w = jnp.concatenate([r[b, :, :, cols].reshape(128, 384) for r, b in w_parts], axis=0)
            prod = jnp.dot(ht, w, preferred_element_type=jnp.float32)
            if fresh:
                acc[:, cols] = prod
            else:
                acc[:, cols] += prod

    take([ga[y], gb[z]], [(wa, y), (wb, z)], True)
    def take_pair(s):
        for buf, w, at in ((ga, wa, y), (gb, wb, z)):
            b1, b2 = (at + s) % RING, (at + RING - s) % RING
            take([buf[b1], buf[b2]], [(w, b1), (w, b2)], False)

    for p in range(len(PARTS)):
        pass_on(p)
    arrived(0)
    take_pair(1)
    take_pair(2)
    arrived(2)
    take_pair(3)
    arrived(3)
    far_y, far_z = (y + 4) % RING, (z + 4) % RING
    take([ga[far_y], gb[far_z]], [(wa, far_y), (wb, far_z)], False)

    order = (2, 1, 3, 0)
    sq_own[...] = jnp.sum(sq[...], axis=0, keepdims=True)
    pair_sq = pltpu.make_async_remote_copy(
        sq_own, sq_in.at[0], sq_s.at[0], sq_r.at[0], device_id=sibling, device_id_type=MESH)
    pair_sq.start()
    pair_copies, x_copies, x_sq = [], [], []
    for i, d in enumerate(order):
        pair_copies.append(pltpu.make_async_remote_copy(
            part.at[i], landed.at[i], rs_s.at[i], rs_r.at[i], device_id=sibling, device_id_type=MESH))
        if d:
            x_copies.append(pltpu.make_async_remote_copy(
                part.at[4 + i], landed.at[4 + i], rs_s.at[4 + i], rs_r.at[4 + i],
                device_id=x_peer(d), device_id_type=MESH))
            x_sq.append(pltpu.make_async_remote_copy(
                sq_pair, sq_in.at[d], sq_s.at[d], sq_r.at[d],
                device_id=x_peer(d), device_id_type=MESH))

    def rows_of(d, side):
        return pl.ds((2 * ((x + d) % 4) + side) * own, own)

    for i, d in enumerate(order):
        part[i] = acc[rows_of(d, 1 - core), :].astype(jnp.bfloat16)
        pair_copies[i].start()
    pair_sq.wait_recv()
    sq_pair[...] = sq_own[...] + sq_in[0]
    for c in x_sq:
        c.start()
    for i, d in enumerate(order):
        pair_copies[i].wait_recv()
        both = acc[rows_of(d, core), :] + landed[i].astype(jnp.float32)
        if d:
            part[4 + i] = both.astype(jnp.bfloat16)
            x_copies[i].start()
        else:
            mine[...] = both

    row8 = lax.broadcasted_iota(jnp.int32, (own, 8), 0)
    lane6 = lax.broadcasted_iota(jnp.int32, (own, 6), 1)
    row6 = lax.broadcasted_iota(jnp.int32, (own, 6), 0)
    row1 = row8[:, :1]
    place = jnp.zeros((own, 1), jnp.int32)
    length = jnp.zeros((own, 1), jnp.int32)
    limit = jnp.zeros((own, 1), jnp.int32)
    token6 = jnp.zeros((own, 6), jnp.int32)
    for r in range(8):
        inside = (row1 >= 6 * r) & (row1 < 6 * r + 6)
        place = jnp.where(inside, row1 - 6 * r, place)
        length = jnp.where(inside, length_ref[r], length)
        limit = jnp.where(inside, accepted_ref[r], limit)
        token6 = jnp.where(row6 == lane6 + 6 * r, jnp.broadcast_to(tok_ref[pl.ds(r, 1), :], (own, 6)), token6)
    token = jnp.sum(token6.astype(jnp.float32), axis=1, keepdims=True).astype(jnp.int32)
    unit = lax.broadcasted_iota(jnp.int32, (own, HD), 1)
    half = jnp.where(unit >= HD // 2, unit - HD // 2, unit).astype(jnp.float32)
    frequency = jnp.exp(half * jnp.float32(-2.0 / HD * 13.122363377404328))
    angle = (length + place).astype(jnp.float32) * frequency
    cosine = jnp.cos(angle)
    sine = jnp.where(unit < HD // 2, -jnp.sin(angle), jnp.sin(angle))

    for c in x_sq:
        c.wait_recv()
    squares = sq_pair[...] + sq_in[1] + sq_in[2] + sq_in[3]
    scale_row = lax.rsqrt(squares / D + 1e-05)
    lane = lax.broadcasted_iota(jnp.int32, (own, rows), 1)
    sub = lax.broadcasted_iota(jnp.int32, (own, rows), 0)
    scale = jnp.sum(jnp.where(lane == sub + sec * own, scale_row, 0.0), axis=1, keepdims=True)

    total = mine[...]
    for i in range(3):
        x_copies[i].wait_recv()
        total = total + landed[4 + i].astype(jnp.float32)
    full = jnp.where(scale == 0.0, 0.0, total * scale)
    logits = full[:, :vocab]
    query = full[:, vocab:]
    ids = lax.broadcasted_iota(jnp.int32, (own, vocab), 1) + tgt * vocab
    picked = jnp.sum(jnp.where(ids == token, logits, 0.0), axis=1, keepdims=True)
    exps = jnp.sum(jnp.exp(logits), axis=1, keepdims=True)
    eye = lax.broadcasted_iota(jnp.int32, (own, 128), 0) == lax.broadcasted_iota(jnp.int32, (own, 128), 1)
    exp_row = jnp.sum(jnp.where(eye, exps, 0.0), axis=0, keepdims=True)
    pick_row = jnp.sum(jnp.where(eye, picked, 0.0), axis=0, keepdims=True)
    msg1[0:1] = exp_row
    msg1[1:2] = pick_row

    def exchange(msg, inbox, at, peer, ssem, rsem):
        copies = [pltpu.make_async_remote_copy(
            msg, inbox.at[at], ssem.at[d], rsem.at[d], device_id=peer(d), device_id_type=MESH)
            for d in range(1, RING)]
        for c in copies:
            c.start()
        inbox[at] = msg[...]
        return copies

    e1 = exchange(msg1, in1, z, z_peer, e1s, e1r)
    rotated = query * cosine + pltpu.roll(query, HD // 2, 1) * sine
    dq_ref[...] = jnp.where(place < limit, rotated, 0.0).astype(jnp.bfloat16)
    for c in e1:
        c.wait_recv()
    msg2[...] = jnp.sum(in1[...], axis=0)
    e2 = exchange(msg2, in2, y, y_peer, e2s, e2r)
    for c in e2:
        c.wait_recv()
    sums = jnp.sum(in2[...], axis=0)
    lp_row = sums[1:2] - jnp.log(sums[0:1])
    sub8 = lax.broadcasted_iota(jnp.int32, (8, 128), 0)
    lane8 = lax.broadcasted_iota(jnp.int32, (8, 128), 1)
    out_lane = lax.broadcasted_iota(jnp.int32, (8, 6), 1)
    out = jnp.zeros((8, 6), jnp.float32)
    for p in range(6):
        col = jnp.sum(jnp.where(lane8 == 6 * sub8 + p, lp_row, 0.0), axis=1, keepdims=True)
        out = jnp.where(out_lane == p, col, out)
    lp_ref[...] = out

    for c in sum(first.values(), []) + sum([sum(g, []) for g in second], []) + [pair_sq] + x_sq + pair_copies + x_copies + e1 + e2:
        c.wait_send()


def local(
    hidden, norm_gain, vocab_weight, draft_gain, query_weight, draft_tokens, accepted, cache_lengths
):
    rows, vocab = hidden.shape[0], vocab_weight.shape[1]
    wide = vocab + HD
    depth = vocab_weight.shape[0]
    own = rows // RING
    any_spec = pl.BlockSpec(memory_space=pl.ANY)
    vmem, smem = pl.BlockSpec(memory_space=pltpu.VMEM), pl.BlockSpec(memory_space=pltpu.SMEM)
    bf16, f32 = jnp.bfloat16, jnp.float32
    dma = pltpu.SemaphoreType.DMA
    lp, dq = pl.pallas_call(
        kernel,
        out_shape=(
            pltpu.VMEM(draft_tokens.shape, f32),
            pltpu.VMEM((own, HD), bf16),
        ),
        in_specs=[any_spec] * 5 + [vmem, smem, smem],
        out_specs=(vmem, vmem),
        scratch_shapes=[
            pltpu.VMEM((8, 8, 16, rows), bf16),
            pltpu.VMEM((8, 8, 16, rows), bf16),
            pltpu.VMEM((depth, wide), bf16),
            pltpu.VMEM((8, 8, 16, wide), bf16),
            pltpu.VMEM((8, 8, 16, wide), bf16),
            pltpu.VMEM((rows, wide), f32),
            pltpu.VMEM((own, wide), f32),
            pltpu.VMEM((8, own, wide), bf16),
            pltpu.VMEM((8, own, wide), bf16),
            pltpu.VMEM((8, rows), f32),
            pltpu.VMEM((1, rows), f32),
            pltpu.VMEM((1, rows), f32),
            pltpu.VMEM((4, 1, rows), f32),
            pltpu.VMEM((2, 16, 128), bf16),
            pltpu.VMEM((2, 128), f32),
            pltpu.VMEM((2, 128), f32),
            pltpu.VMEM((8, 2, 128), f32),
            pltpu.VMEM((8, 2, 128), f32),
            dma((6,)),
            dma((2, 8)), dma((2, 8)),
            dma((len(PARTS), 2, 2, 4)), dma((len(PARTS), 2, 2, 4)),
            dma((8,)), dma((8,)),
            dma((8,)), dma((8,)),
            dma((8,)), dma((8,)),
            dma((8,)), dma((8,)),
        ],
        compiler_params=pltpu.CompilerParams(
            collective_id=0, has_side_effects=True, vmem_limit_bytes=60 * 1024 * 1024
        ),
    )(
        hidden.T,
        norm_gain.reshape(16, 128),
        vocab_weight,
        draft_gain.reshape(128, 128),
        query_weight,
        draft_tokens,
        accepted,
        cache_lengths,
    )
    return lp, dq


def solution(mesh):
    return jax.shard_map(
        local,
        mesh=mesh,
        in_specs=(
            P(None, ("sec", "tgt")),
            P("sec"),
            P("sec", "tgt"),
            P(),
            P("sec", "tgt"),
            P("sec", None),
            P("sec"),
            P("sec"),
        ),
        out_specs=(P("sec", None), P("sec", "tgt")),
        check_vma=False,
    )
```

```python
import jax
import jax.numpy as jnp
from jax import lax
from jax.experimental import pallas as pl
from jax.experimental.pallas import tpu as pltpu
from jax.sharding import PartitionSpec as P

D = 16384
HD = 128
RING = 8
MESH = pl.DeviceIdType.MESH
SLOT = (0, 1, 3, 5, 7, 6, 4, 2)
PARTS = ((0, 3, 2), (3, 5, 2))


def kernel(
    h_hbm, gain_hbm, w_hbm, dgain_hbm, wq_hbm, tok_ref, accepted_ref, length_ref,
    lp_ref, dq_ref,
    ga, gb, raw, wa, wb, acc, mine, part, landed, sq, sq_own, sq_pair, sq_in, gains, msg1, msg2, in1, in2,
    local_sem, p1s, p1r, p2s, p2r, rs_s, rs_r, sq_s, sq_r, e1s, e1r, e2s, e2r,
):
    tgt = lax.axis_index("tgt")
    sec = lax.axis_index("sec")
    y, z = tgt // RING, tgt % RING
    rows, vocab = 384, w_hbm.shape[1]
    own = rows // RING

    def z_peer(d):
        return (y * RING + (z + d) % RING, sec)

    def y_peer(d):
        return (((y + d) % RING) * RING + z, sec)

    x, core = sec // 2, sec % 2
    sibling = (tgt, 2 * x + 1 - core)

    def x_peer(d):
        return (tgt, 2 * ((x + d) % 4) + core)

    barrier = pltpu.get_barrier_semaphore()
    for d in (4, 3, 5, 2, 6, 1, 7):
        for peer in (z_peer(d), y_peer(d)):
            pl.semaphore_signal(barrier, inc=1, device_id=peer, device_id_type=MESH)
    for peer in (sibling, x_peer(1), x_peer(2), x_peer(3)):
        pl.semaphore_signal(barrier, inc=1, device_id=peer, device_id_type=MESH)

    w_copies = [
        pltpu.make_async_copy(w_hbm, raw.at[:, pl.ds(0, vocab)], local_sem.at[0]),
        pltpu.make_async_copy(wq_hbm, raw.at[:, pl.ds(vocab, HD)], local_sem.at[1]),
        pltpu.make_async_copy(gain_hbm, gains.at[0], local_sem.at[2]),
        pltpu.make_async_copy(dgain_hbm.at[pl.ds(sec * 16, 16)], gains.at[1], local_sem.at[3]),
    ]
    h_copies = [
        pltpu.make_async_copy(h_hbm.at[pl.ds(0, 16)], ga.at[y, 0], local_sem.at[4]),
        pltpu.make_async_copy(h_hbm.at[pl.ds(16, 16)], gb.at[z, 0], local_sem.at[5]),
    ]
    for c in h_copies + w_copies:
        c.start()

    pl.semaphore_wait(barrier, 2 * (RING - 1) + 4)

    def first_copies(d):
        to = SLOT[RING - d]
        return [
            pltpu.make_async_remote_copy(
                h_hbm.at[pl.ds(0, 16)], ga.at[y, to], p1s.at[0, d], p1r.at[0, d],
                device_id=z_peer(d), device_id_type=MESH),
            pltpu.make_async_remote_copy(
                h_hbm.at[pl.ds(16, 16)], gb.at[z, to], p1s.at[1, d], p1r.at[1, d],
                device_id=y_peer(d), device_id_type=MESH),
        ]

    first = {d: first_copies(d) for d in range(1, RING)}
    for d in (1, 7, 2, 6, 3, 5, 4):
        for c in first[d]:
            c.start()

    def ring_copies(p):
        at_slot, count, up = PARTS[p]
        near, far, third, fourth = [], [], [], []
        for k, (buf, at, peer) in enumerate(((ga, y, y_peer), (gb, z, z_peer))):
            for way in (0, 1):
                step = 1 if way == 0 else RING - 1
                from2 = (at + 2 * (RING - step)) % RING
                lo, n = (at_slot, up) if way == 0 else (at_slot + up, count - up)
                for kind, (group, ref, hops) in enumerate((
                    (near, buf.at[at, pl.ds(at_slot, count)], step),
                    (far, buf.at[at, pl.ds(at_slot, count)], 2 * step),
                    (third, buf.at[from2, pl.ds(at_slot, count)], step),
                    (fourth, buf.at[from2, pl.ds(lo, n)] if n else None, 2 * step),
                )):
                    if ref is not None:
                        group.append(pltpu.make_async_remote_copy(
                            ref, ref, p2s.at[p, k, way, kind], p2r.at[p, k, way, kind],
                            device_id=peer(hops), device_id_type=MESH))
        return near, far, third, fourth

    second = [ring_copies(p) for p in range(len(PARTS))]

    def spread(p):
        near, far = second[p][:2]
        for k in (0, 1):
            for slot in range(PARTS[p][0], PARTS[p][0] + PARTS[p][1]):
                if slot > 0:
                    first[RING - SLOT.index(slot)][k].wait_recv()
            for c in far[2 * k:2 * k + 2] + near[2 * k:2 * k + 2]:
                c.start()

    def pass_on(p):
        near, far, third, fourth = second[p]
        for came, on4, on3 in zip(far, fourth, third):
            came.wait_recv()
            on4.start()
            on3.start()

    def arrived(kind):
        for group in second:
            for c in group[kind]:
                c.wait_recv()

    for c in h_copies:
        c.wait()
    for p in range(len(PARTS)):
        spread(p)

    for c in w_copies:
        c.wait()

    def slot_of(rel):
        return jnp.where(rel == 0, 0, jnp.where(rel <= 4, 2 * rel - 1, 16 - 2 * rel))

    gt = jnp.transpose(gains[0].astype(jnp.float32))
    dgt = jnp.transpose(gains[1].astype(jnp.float32))
    for j in range(16):
        span = pl.ds(128 * j, 128)
        left = (raw[span, pl.ds(0, vocab)].astype(jnp.float32) * gt[:, j:j + 1]).astype(jnp.bfloat16)
        right = (raw[span, pl.ds(vocab, HD)].astype(jnp.float32) * dgt[:, j:j + 1]).astype(jnp.bfloat16)
        for i in range(4):
            yy, zz = j // 2, 4 * (j % 2) + i
            for wide, values in ((pl.ds(0, vocab), left), (pl.ds(vocab, HD), right)):
                wa[yy, slot_of((zz + RING - z) % RING), :, wide] = values[32 * i:32 * i + 16]
                wb[zz, slot_of((yy + RING - y) % RING), :, wide] = values[32 * i + 16:32 * i + 32]

    def take(h_parts, w_parts, fresh):
        h = jnp.concatenate([v.reshape(128, rows) for v in h_parts], axis=0)
        hf = h.astype(jnp.float32)
        squares = jnp.sum((hf * hf).reshape(32, 8, rows), axis=0)
        sq[...] = squares if fresh else sq[...] + squares
        ht = jnp.transpose(h)
        for n in range(3):
            cols = pl.ds(n * 384, 384)
            w = jnp.concatenate([r[b, :, :, cols].reshape(128, 384) for r, b in w_parts], axis=0)
            prod = jnp.dot(ht, w, preferred_element_type=jnp.float32)
            if fresh:
                acc[:, cols] = prod
            else:
                acc[:, cols] += prod

    take([ga[y], gb[z]], [(wa, y), (wb, z)], True)
    def take_pair(s):
        for buf, w, at in ((ga, wa, y), (gb, wb, z)):
            b1, b2 = (at + s) % RING, (at + RING - s) % RING
            take([buf[b1], buf[b2]], [(w, b1), (w, b2)], False)

    for p in range(len(PARTS)):
        pass_on(p)
    arrived(0)
    take_pair(1)
    take_pair(2)
    arrived(2)
    take_pair(3)
    arrived(3)
    far_y, far_z = (y + 4) % RING, (z + 4) % RING
    take([ga[far_y], gb[far_z]], [(wa, far_y), (wb, far_z)], False)

    order = (2, 1, 3, 0)
    sq_own[...] = jnp.sum(sq[...], axis=0, keepdims=True)
    pair_sq = pltpu.make_async_remote_copy(
        sq_own, sq_in.at[0], sq_s.at[0], sq_r.at[0], device_id=sibling, device_id_type=MESH)
    pair_sq.start()
    pair_copies, x_copies, x_sq = [], [], []
    for i, d in enumerate(order):
        pair_copies.append(pltpu.make_async_remote_copy(
            part.at[i], landed.at[i], rs_s.at[i], rs_r.at[i], device_id=sibling, device_id_type=MESH))
        if d:
            x_copies.append(pltpu.make_async_remote_copy(
                part.at[4 + i], landed.at[4 + i], rs_s.at[4 + i], rs_r.at[4 + i],
                device_id=x_peer(d), device_id_type=MESH))
            x_sq.append(pltpu.make_async_remote_copy(
                sq_pair, sq_in.at[d], sq_s.at[d], sq_r.at[d],
                device_id=x_peer(d), device_id_type=MESH))

    def rows_of(d, side):
        return pl.ds((2 * ((x + d) % 4) + side) * own, own)

    for i, d in enumerate(order):
        part[i] = acc[rows_of(d, 1 - core), :].astype(jnp.bfloat16)
        pair_copies[i].start()
    pair_sq.wait_recv()
    sq_pair[...] = sq_own[...] + sq_in[0]
    for c in x_sq:
        c.start()
    for i, d in enumerate(order):
        pair_copies[i].wait_recv()
        both = acc[rows_of(d, core), :] + landed[i].astype(jnp.float32)
        if d:
            part[4 + i] = both.astype(jnp.bfloat16)
            x_copies[i].start()
        else:
            mine[...] = both

    row8 = lax.broadcasted_iota(jnp.int32, (own, 8), 0)
    lane6 = lax.broadcasted_iota(jnp.int32, (own, 6), 1)
    row6 = lax.broadcasted_iota(jnp.int32, (own, 6), 0)
    row1 = row8[:, :1]
    place = jnp.zeros((own, 1), jnp.int32)
    length = jnp.zeros((own, 1), jnp.int32)
    limit = jnp.zeros((own, 1), jnp.int32)
    token6 = jnp.zeros((own, 6), jnp.int32)
    for r in range(8):
        inside = (row1 >= 6 * r) & (row1 < 6 * r + 6)
        place = jnp.where(inside, row1 - 6 * r, place)
        length = jnp.where(inside, length_ref[r], length)
        limit = jnp.where(inside, accepted_ref[r], limit)
        token6 = jnp.where(row6 == lane6 + 6 * r, jnp.broadcast_to(tok_ref[pl.ds(r, 1), :], (own, 6)), token6)
    token = jnp.sum(token6.astype(jnp.float32), axis=1, keepdims=True).astype(jnp.int32)
    unit = lax.broadcasted_iota(jnp.int32, (own, HD), 1)
    half = jnp.where(unit >= HD // 2, unit - HD // 2, unit).astype(jnp.float32)
    frequency = jnp.exp(half * jnp.float32(-2.0 / HD * 13.122363377404328))
    angle = (length + place).astype(jnp.float32) * frequency
    cosine = jnp.cos(angle)
    sine = jnp.where(unit < HD // 2, -jnp.sin(angle), jnp.sin(angle))

    for c in x_sq:
        c.wait_recv()
    squares = sq_pair[...] + sq_in[1] + sq_in[2] + sq_in[3]
    scale_row = lax.rsqrt(squares / D + 1e-05)
    lane = lax.broadcasted_iota(jnp.int32, (own, rows), 1)
    sub = lax.broadcasted_iota(jnp.int32, (own, rows), 0)
    scale = jnp.sum(jnp.where(lane == sub + sec * own, scale_row, 0.0), axis=1, keepdims=True)

    total = mine[...]
    for i in range(3):
        x_copies[i].wait_recv()
        total = total + landed[4 + i].astype(jnp.float32)
    full = jnp.where(scale == 0.0, 0.0, total * scale)
    logits = full[:, :vocab]
    query = full[:, vocab:]
    ids = lax.broadcasted_iota(jnp.int32, (own, vocab), 1) + tgt * vocab
    picked = jnp.sum(jnp.where(ids == token, logits, 0.0), axis=1, keepdims=True)
    exps = jnp.sum(jnp.exp(logits), axis=1, keepdims=True)
    eye = lax.broadcasted_iota(jnp.int32, (own, 128), 0) == lax.broadcasted_iota(jnp.int32, (own, 128), 1)
    exp_row = jnp.sum(jnp.where(eye, exps, 0.0), axis=0, keepdims=True)
    pick_row = jnp.sum(jnp.where(eye, picked, 0.0), axis=0, keepdims=True)
    msg1[0:1] = exp_row
    msg1[1:2] = pick_row

    def exchange(msg, inbox, at, peer, ssem, rsem):
        copies = [pltpu.make_async_remote_copy(
            msg, inbox.at[at], ssem.at[d], rsem.at[d], device_id=peer(d), device_id_type=MESH)
            for d in range(1, RING)]
        for c in copies:
            c.start()
        inbox[at] = msg[...]
        return copies

    e1 = exchange(msg1, in1, z, z_peer, e1s, e1r)
    rotated = query * cosine + pltpu.roll(query, HD // 2, 1) * sine
    dq_ref[...] = jnp.where(place < limit, rotated, 0.0).astype(jnp.bfloat16)
    for c in e1:
        c.wait_recv()
    msg2[...] = jnp.sum(in1[...], axis=0)
    e2 = exchange(msg2, in2, y, y_peer, e2s, e2r)
    for c in e2:
        c.wait_recv()
    sums = jnp.sum(in2[...], axis=0)
    lp_row = sums[1:2] - jnp.log(sums[0:1])
    sub8 = lax.broadcasted_iota(jnp.int32, (8, 128), 0)
    lane8 = lax.broadcasted_iota(jnp.int32, (8, 128), 1)
    out_lane = lax.broadcasted_iota(jnp.int32, (8, 6), 1)
    out = jnp.zeros((8, 6), jnp.float32)
    for p in range(6):
        col = jnp.sum(jnp.where(lane8 == 6 * sub8 + p, lp_row, 0.0), axis=1, keepdims=True)
        out = jnp.where(out_lane == p, col, out)
    lp_ref[...] = out

    for c in sum(first.values(), []) + sum([sum(g, []) for g in second], []) + [pair_sq] + x_sq + pair_copies + x_copies + e1 + e2:
        c.wait_send()


def local(
    hidden, norm_gain, vocab_weight, draft_gain, query_weight, draft_tokens, accepted, cache_lengths
):
    rows, vocab = hidden.shape[0], vocab_weight.shape[1]
    wide = vocab + HD
    depth = vocab_weight.shape[0]
    own = rows // RING
    any_spec = pl.BlockSpec(memory_space=pl.ANY)
    vmem, smem = pl.BlockSpec(memory_space=pltpu.VMEM), pl.BlockSpec(memory_space=pltpu.SMEM)
    bf16, f32 = jnp.bfloat16, jnp.float32
    dma = pltpu.SemaphoreType.DMA
    lp, dq = pl.pallas_call(
        kernel,
        out_shape=(
            pltpu.VMEM(draft_tokens.shape, f32),
            pltpu.VMEM((own, HD), bf16),
        ),
        in_specs=[any_spec] * 5 + [vmem, smem, smem],
        out_specs=(vmem, vmem),
        scratch_shapes=[
            pltpu.VMEM((8, 8, 16, rows), bf16),
            pltpu.VMEM((8, 8, 16, rows), bf16),
            pltpu.VMEM((depth, wide), bf16),
            pltpu.VMEM((8, 8, 16, wide), bf16),
            pltpu.VMEM((8, 8, 16, wide), bf16),
            pltpu.VMEM((rows, wide), f32),
            pltpu.VMEM((own, wide), f32),
            pltpu.VMEM((8, own, wide), bf16),
            pltpu.VMEM((8, own, wide), bf16),
            pltpu.VMEM((8, rows), f32),
            pltpu.VMEM((1, rows), f32),
            pltpu.VMEM((1, rows), f32),
            pltpu.VMEM((4, 1, rows), f32),
            pltpu.VMEM((2, 16, 128), bf16),
            pltpu.VMEM((2, 128), f32),
            pltpu.VMEM((2, 128), f32),
            pltpu.VMEM((8, 2, 128), f32),
            pltpu.VMEM((8, 2, 128), f32),
            dma((6,)),
            dma((2, 8)), dma((2, 8)),
            dma((len(PARTS), 2, 2, 4)), dma((len(PARTS), 2, 2, 4)),
            dma((8,)), dma((8,)),
            dma((8,)), dma((8,)),
            dma((8,)), dma((8,)),
            dma((8,)), dma((8,)),
        ],
        compiler_params=pltpu.CompilerParams(
            collective_id=0, has_side_effects=True, vmem_limit_bytes=60 * 1024 * 1024
        ),
    )(
        hidden.T,
        norm_gain.reshape(16, 128),
        vocab_weight,
        draft_gain.reshape(128, 128),
        query_weight,
        draft_tokens,
        accepted,
        cache_lengths,
    )
    return lp, dq


def solution(mesh):
    return jax.shard_map(
        local,
        mesh=mesh,
        in_specs=(
            P(None, ("sec", "tgt")),
            P("sec"),
            P("sec", "tgt"),
            P(),
            P("sec", "tgt"),
            P("sec", None),
            P("sec"),
            P("sec"),
        ),
        out_specs=(P("sec", None), P("sec", "tgt")),
        check_vma=False,
    )
```
